256 devices in a mesh: vocab: 16 (over x, y), dp: 16 (over z, core).
Axes of the slice: x: 4, y: 4, z: 8, core: 2. Of those that a mesh axis runs over, the one named last changes fastest.
Arguments:
- hidden: bfloat16 [512, 5120], P('dp')
- table: bfloat16 [131072, 5120], P(('vocab', 'dp'))
- embed_grad: bfloat16 [512, 5120], P('dp'), may hold values from -1.1953125 to 1.1953125
- token_ids: int32 [512], P('dp'), may hold values from 0 to 131071
- target_ids: int32 [512], P('dp'), may hold values from 0 to 131071
Outputs:
- grad_hidden: bfloat16 [512, 5120], P('dp', 'vocab')
- grad_table: bfloat16 [131072, 5120], P(('vocab', 'dp'))
- loss_sum: float32 [], replicated
The draws below stay inside these ranges and needn't reach their ends.
All inputs are finite; a program needn't handle non-finite values.
Results may differ from the reference program's by a relative error of at most 0.0037.
Values may be sent and summed in bfloat16 or wider, within the bound.
No kernel may reach another device: no remote copies, remote signals or barrier semaphores. Data moves between devices by JAX's collectives and lax.ppermute only.
A program may use at most 128 MiB of HBM per device.

```python
import math
import jax
import jax.numpy as jnp
import numpy as np
from jax import lax

D = 5120
VOC_DEV = 512
VOCAB = 131072
TOKENS = 512


def table_rows(key, row_ids, scale_lo, scale_hi):

    def one_row(row_id):
        row_key = jax.random.fold_in(key, row_id)
        value_key, scale_key = jax.random.split(row_key)
        values = jax.random.normal(value_key, (D,), jnp.float32)
        log_scale = jax.random.uniform(scale_key, (), jnp.float32, math.log(scale_lo), math.log(scale_hi))
        return values * jnp.exp(log_scale) * (math.sqrt(3.0) * D ** (-0.25))
    return jax.vmap(one_row)(row_ids)


def draw_table(key, part):
    scale_lo, scale_hi = (1.0, 1.0)
    blocks = jnp.arange(VOCAB, dtype=jnp.int32).reshape(VOCAB // VOC_DEV, VOC_DEV)
    out_rows = lax.map(lambda block: table_rows(key, block, scale_lo, scale_hi).astype(jnp.bfloat16), blocks)
    return out_rows.reshape(VOCAB, D)


def draw_hidden(key, part):
    own_key = jax.random.fold_in(key, 11)
    values = jax.random.normal(own_key, (TOKENS, D), jnp.float32) * (math.sqrt(3.0) * D ** (-0.25))
    return values.astype(jnp.bfloat16)


def with_ends(result, rng, smallest, top_value):
    spot = [jax.random.randint(jax.random.fold_in(rng, axis), (), 0, length) for axis, length in enumerate(result.shape)]
    main_axis = result.shape.index(max(result.shape))
    beside = spot[:main_axis] + [(spot[main_axis] + 1) % result.shape[main_axis]] + spot[main_axis + 1:]
    return result.at[tuple(spot)].set(smallest).at[tuple(beside)].set(top_value)


def shard_levels(key, extent, pieces, low, largest):
    factor_of, own = 1.0, jax.random.fold_in(key, 6)
    for position, blocks in pieces:
        heights = jnp.exp(jax.random.uniform(jax.random.fold_in(own, position), (blocks,), jnp.float32, low / len(pieces), largest / len(pieces)))
        factor_of = factor_of * jnp.repeat(heights, extent[position] // blocks).reshape([-1 if axis == position else 1 for axis in range(len(extent))])
    return factor_of


def wide_ids(rng, dims, count, skew):
    loads = [min(1 << octave, count + 1 - (1 << octave)) * (1 << 20) // math.isqrt((1 << octave) ** skew) + 1 for octave in range((count + 1).bit_length()) if 1 << octave <= count]
    deviation = 1 + sum(loads) // (1 << 30)
    grid = np.cumsum(np.array([max(1, weight // deviation) for weight in loads]))
    pick = jax.random.randint(jax.random.fold_in(rng, 1), dims, 0, int(grid[len(loads) - 1]))
    start = jnp.left_shift(1, jnp.searchsorted(jnp.asarray(grid, jnp.int32), pick, side="right").astype(jnp.int32))
    rank = start - 1 + jax.random.randint(jax.random.fold_in(rng, 4), dims, 0, 1 << 30) % jnp.minimum(start, count + 1 - start)
    return jax.random.permutation(jax.random.fold_in(rng, 2), count)[rank].astype(jnp.int32)


def centred(key, shape, deviation, limit, cuts=(), kind=jnp.bfloat16):
    values = jax.random.normal(key, shape, jnp.float32) * deviation
    if len(cuts) > 0:
        values = shard_levels(key, shape, cuts, -0.22, 0.18) * values
    return jnp.clip(values, min=-limit, max=limit).astype(kind)


def setup_inputs(seed: int = 0) -> dict:
    seeds = jax.random.split(jax.random.key(seed), 6)
    return {
        "hidden": draw_hidden(jax.random.fold_in(seeds[5], 71), 0),
        "table": draw_table(jax.random.fold_in(seeds[5], 71), 0),
        "embed_grad": centred(seeds[2], (TOKENS, D), 0.2, 1.1953125, ((0, 16),)),
        "token_ids": with_ends(wide_ids(seeds[3], (TOKENS,), VOCAB, 2), jax.random.fold_in(seeds[3], 3), 0, VOCAB - 1).astype(jnp.int32),
        "target_ids": with_ends(wide_ids(seeds[4], (TOKENS,), VOCAB, 2), jax.random.fold_in(seeds[4], 3), 0, VOCAB - 1).astype(jnp.int32),
    }


def reference(hidden, table, embed_grad, token_ids, target_ids):
    logits = jnp.dot(hidden, table.T, preferred_element_type=jnp.float32)
    row_top = jnp.max(logits, axis=1)
    shifted = jnp.exp(logits - row_top[:, None])
    row_total = jnp.sum(shifted, axis=1)
    columns = jnp.arange(VOCAB, dtype=jnp.int32)
    target_hit = columns[None, :] == target_ids[:, None]
    target_logit = jnp.sum(jnp.where(target_hit, logits, jnp.float32(0.0)), axis=1)
    loss_sum = jnp.sum(row_top + jnp.log(row_total) - target_logit)
    dlogits = (shifted / row_total[:, None] - target_hit.astype(jnp.float32)).astype(jnp.bfloat16)
    grad_hidden = jnp.dot(dlogits, table, preferred_element_type=jnp.float32).astype(jnp.bfloat16)
    block_rows = VOC_DEV * 16
    block_count = VOCAB // block_rows

    def table_block(block_index):
        offset = (block_index * block_rows).astype(jnp.int32)
        dl_block = lax.dynamic_slice_in_dim(dlogits, offset, block_rows, 1)
        head_grad = jnp.dot(dl_block.T, hidden, preferred_element_type=jnp.float32)
        block_cols = offset + jnp.arange(block_rows, dtype=jnp.int32)
        onehot_tok = (token_ids[:, None] == block_cols[None, :]).astype(jnp.bfloat16)
        embed_term = jnp.dot(onehot_tok.T, embed_grad, preferred_element_type=jnp.float32)
        return (head_grad + embed_term).astype(jnp.bfloat16)

    blocks = lax.map(table_block, jnp.arange(block_count, dtype=jnp.int32))
    grad_table = blocks.reshape(VOCAB, D)
    return grad_hidden, grad_table, loss_sum
```

```python
import functools

import jax
import jax.numpy as jnp
from jax import lax
from jax.experimental import pallas as pl
from jax.experimental.pallas import tpu as pltpu
from jax.sharding import Mesh
from jax.sharding import PartitionSpec as P

XY = ("x", "y")
XYZ = ("x", "y", "z")
ALL = ("x", "y", "z", "c")
F32 = jnp.float32
BF16 = jnp.bfloat16
CHUNK = 512
LIMIT = 48 * 1024 * 1024


def _params():
    return pltpu.CompilerParams(vmem_limit_bytes=LIMIT)


def _cost(flops, moved):
    return pl.CostEstimate(flops=flops, bytes_accessed=moved, transcendentals=0)


def _const(*zeros):
    return lambda i: zeros


def _row_ids(pos_ref, rows, tokens):
    at = lax.broadcasted_iota(jnp.int32, (2 * rows, tokens), 0)
    return jnp.where(at < rows, pos_ref[1] + at, pos_ref[2] + at - rows)


def _logits_kernel(steps, rows, pos_ref, tgt_ref, *refs):
    pieces, (own_ref, oth_ref, logit_ref, hid_ref, stat_ref) = refs[:-5], refs[-5:]
    step = pl.program_id(0)
    h = jnp.concatenate([p[...] for p in pieces], axis=0)
    hid_ref[...] = h
    dims = (((1,), (1,)), ((), ()))
    a = lax.dot_general(own_ref[...], h, dims, preferred_element_type=F32)
    b = lax.dot_general(oth_ref[...], h, dims, preferred_element_type=F32)

    @pl.when(step == 0)
    def _():
        logit_ref[:rows] = a
        logit_ref[rows:] = b

    @pl.when(step > 0)
    def _():
        logit_ref[:rows] += a
        logit_ref[rows:] += b

    @pl.when(step == steps - 1)
    def _():
        z = pos_ref[0]
        logit = logit_ref[...]
        tokens = logit.shape[1]
        block = tokens // 8
        tgt = pltpu.roll(jnp.broadcast_to(tgt_ref[...], (8, tokens)), lax.rem(8 - z, 8) * block, 1)[:1]
        top = jnp.max(logit, axis=0, keepdims=True)
        total = jnp.sum(jnp.exp(logit - top), axis=0, keepdims=True)
        hit = _row_ids(pos_ref, rows, tokens) == tgt
        own = jnp.sum(jnp.where(hit, logit, 0.0), axis=0, keepdims=True)
        stack = jnp.concatenate([top, total, own, jnp.zeros((5, tokens), F32)], axis=0)
        stat_ref[...] = pltpu.roll(stack, z * block, 1)


def _grad_hidden_kernel(rows, pos_ref, stat_ref, tgt_ref, logit_ref, own_ref, oth_ref, part_ref, dl_ref, loss_ref, dl_t):
    step = pl.program_id(0)

    @pl.when(step == 0)
    def _():
        z = pos_ref[0]
        tokens = logit_ref.shape[1]
        block = tokens // 8
        back = lax.rem(8 - z, 8) * block
        tops = stat_ref[:, 0:2, :]
        sums = stat_ref[:, 2:4, :]
        top = jnp.max(tops, axis=0)
        total = jnp.sum(sums * jnp.exp(tops - top[None]), axis=0)
        hit_sum = jnp.sum(stat_ref[:, 4:6, :], axis=0)
        loss_ref[...] = jnp.sum(top + jnp.log(total) - hit_sum, keepdims=True)

        def rolled(v):
            flat = jnp.concatenate([v[0:1], v[1:2]], axis=1)
            return pltpu.roll(jnp.broadcast_to(flat, (8, tokens)), back, 1)[:1]

        top_row = rolled(top)
        inv_row = rolled(1.0 / total)
        tgt = pltpu.roll(jnp.broadcast_to(tgt_ref[...], (8, tokens)), back, 1)[:1]
        hit = _row_ids(pos_ref, rows, tokens) == tgt
        dl = jnp.exp(logit_ref[...] - top_row) * inv_row - jnp.where(hit, 1.0, 0.0)
        dl_ref[...] = dl.astype(BF16)
        dl_t[...] = dl.T.astype(BF16)

    part = jnp.dot(dl_t[:, :rows], own_ref[...], preferred_element_type=F32)
    part += jnp.dot(dl_t[:, rows:], oth_ref[...], preferred_element_type=F32)
    part_ref[...] = part.T.astype(BF16)


def _sum_kernel(pos_ref, got_ref, out_ref):
    z = pos_ref[0]
    total = jnp.sum(got_ref[...].astype(F32), axis=0).T
    block = total.shape[0] // 8
    for r in range(8):
        out_ref[lax.rem(z + r, 8)] = total[r * block : (r + 1) * block]


def _grad_table_kernel(pos_ref, tok_ref, dl_own_ref, dl_oth_ref, h_own_ref, h_oth_ref, e_ref, out_ref, hot):
    @pl.when(pl.program_id(0) == 0)
    def _():
        at = lax.broadcasted_iota(jnp.int32, hot.shape, 0) + pos_ref[1]
        hot[...] = jnp.where(at == tok_ref[...], 1.0, 0.0).astype(BF16)

    acc = jnp.dot(dl_own_ref[...], h_own_ref[...], preferred_element_type=F32)
    acc += jnp.dot(dl_oth_ref[...], h_oth_ref[...], preferred_element_type=F32)
    acc += jnp.dot(hot[...], e_ref[...], preferred_element_type=F32)
    out_ref[...] = acc.astype(BF16)


def per_device(hidden, table, embed_grad, token_ids, target_ids):
    rows, width = table.shape
    n_tok = hidden.shape[0]
    nz = lax.axis_size("z")
    tokens = n_tok * nz
    xi, yi, zi, ci = (lax.axis_index(a) for a in ALL)
    base = ((xi * 4 + yi) * nz + zi) * 2
    pos = jnp.stack([zi, (base + ci) * rows, (base + 1 - ci) * rows]).astype(jnp.int32)
    swap = [(0, 1), (1, 0)]
    up = [(i, (i + 1) % nz) for i in range(nz)]
    down = [(i, (i - 1) % nz) for i in range(nz)]

    table_oth = lax.ppermute(table, "c", swap)
    u, d, ups, downs = hidden, hidden, [], []
    for _ in range(3):
        u, d = lax.optimization_barrier((lax.ppermute(u, "z", up), lax.ppermute(d, "z", down)))
        ups.append(u)
        downs.append(d)
    half = n_tok // 2
    far = [lax.ppermute(u[:half], "z", up), lax.ppermute(d[half:], "z", down)]
    pieces = [hidden, *downs, *far, *ups[::-1]]

    ids = jnp.concatenate([target_ids, token_ids])
    ids = lax.all_to_all(jnp.broadcast_to(ids[None], (2 * nz, 2 * n_tok)), ("z", "c"), 0, 0, tiled=True)
    targets = lax.dynamic_index_in_dim(ids.reshape(nz, 2, 2 * n_tok), ci, 1, False)[:, :n_tok].reshape(1, tokens)
    toks = ids[:, n_tok:].reshape(1, 2 * tokens)

    steps = width // CHUNK
    smem = pl.BlockSpec(memory_space=pltpu.SMEM)
    col = lambda n: pl.BlockSpec((n, CHUNK), lambda i: (0, i))
    logit, h_own, stat = pl.pallas_call(
        functools.partial(_logits_kernel, steps, rows),
        grid=(steps,),
        in_specs=[smem, pl.BlockSpec((1, tokens), _const(0, 0)), *[col(p.shape[0]) for p in pieces], col(rows), col(rows)],
        out_specs=[
            pl.BlockSpec((2 * rows, tokens), _const(0, 0)),
            col(tokens),
            pl.BlockSpec((8, tokens), _const(0, 0)),
        ],
        out_shape=[
            jax.ShapeDtypeStruct((2 * rows, tokens), F32),
            jax.ShapeDtypeStruct((tokens, width), BF16),
            jax.ShapeDtypeStruct((8, tokens), F32),
        ],
        compiler_params=_params(),
        cost_estimate=_cost(4 * rows * tokens * width, 4 * rows * width + 4 * tokens * width),
        name="logits",
    )(pos, targets, *pieces, table, table_oth)

    e_src, _ = lax.optimization_barrier((embed_grad, far[0]))
    e_all = lax.all_gather(e_src, ("z", "c"), axis=0, tiled=True)

    lanes = 128
    payload = stat[:4].reshape(8, lanes)
    peers = lax.axis_size(XYZ)
    stats = lax.all_to_all(jnp.broadcast_to(payload[None], (peers, 8, lanes)), XYZ, 0, 0, tiled=True)
    h_src, stats = lax.optimization_barrier((h_own, stats))
    h_oth = lax.ppermute(h_src, "c", swap)

    part, dl, loss = pl.pallas_call(
        functools.partial(_grad_hidden_kernel, rows),
        grid=(steps,),
        in_specs=[
            smem,
            pl.BlockSpec((peers, 8, lanes), _const(0, 0, 0)),
            pl.BlockSpec((1, tokens), _const(0, 0)),
            pl.BlockSpec((2 * rows, tokens), _const(0, 0)),
            col(rows),
            col(rows),
        ],
        out_specs=[
            pl.BlockSpec((CHUNK, tokens), lambda i: (i, 0)),
            pl.BlockSpec((2 * rows, tokens), _const(0, 0)),
            pl.BlockSpec((1, 1), _const(0, 0)),
        ],
        out_shape=[
            jax.ShapeDtypeStruct((width, tokens), BF16),
            jax.ShapeDtypeStruct((2 * rows, tokens), BF16),
            jax.ShapeDtypeStruct((1, 1), F32),
        ],
        scratch_shapes=[pltpu.VMEM((tokens, 2 * rows), BF16)],
        compiler_params=_params(),
        cost_estimate=_cost(4 * rows * tokens * width, 4 * rows * width + 2 * tokens * width),
        name="grad_hidden_part",
    )(pos, stats, targets, logit, table, table_oth)

    nxy = lax.axis_size(XY)
    feats = width // nxy
    got = lax.all_to_all(part, XY, 0, 0, tiled=True).reshape(nxy, feats, tokens)
    by_z = pl.pallas_call(
        _sum_kernel,
        in_specs=[smem, pl.BlockSpec(memory_space=pltpu.VMEM)],
        out_specs=pl.BlockSpec(memory_space=pltpu.VMEM),
        out_shape=jax.ShapeDtypeStruct((nz, n_tok, feats), F32),
        compiler_params=_params(),
        cost_estimate=_cost(width * tokens, 2 * width * tokens),
        name="sum_xy",
    )(pos, got)
    by_z = lax.all_to_all(by_z, "z", 0, 0, tiled=True)
    grad_hidden = jnp.sum(by_z, axis=0).astype(BF16)

    dl_oth = lax.ppermute(dl[rows:], "c", swap)
    small = pl.BlockSpec((rows, tokens), _const(0, 0))
    row = pl.BlockSpec((1, 2 * tokens), _const(0, 0))
    grad_table = pl.pallas_call(
        _grad_table_kernel,
        grid=(steps,),
        in_specs=[smem, row, small, small, col(tokens), col(tokens), col(2 * tokens)],
        out_specs=col(rows),
        out_shape=jax.ShapeDtypeStruct((rows, width), BF16),
        scratch_shapes=[pltpu.VMEM((rows, 2 * tokens), BF16)],
        compiler_params=_params(),
        cost_estimate=_cost(8 * rows * tokens * width, 8 * tokens * width + 2 * rows * width),
        name="grad_table",
    )(pos, toks, dl[:rows], dl_oth, h_own, h_oth, e_all)

    loss = loss[0, 0]
    loss = loss + lax.ppermute(loss, "c", swap)
    return grad_hidden, grad_table, loss


def solution(mesh):
    fine = Mesh(mesh.devices.reshape(4, 4, 8, 2), ALL)
    in_specs = (P(("z", "c"), None), P(ALL, None), P(("z", "c"), None), P(("z", "c")), P(("z", "c")))
    out_specs = (P(("z", "c"), XY), P(ALL, None), P())
    return jax.shard_map(per_device, mesh=fine, in_specs=in_specs, out_specs=out_specs, check_vma=False)
```

```python
import functools

import jax
import jax.numpy as jnp
from jax import lax
from jax.experimental import pallas as pl
from jax.experimental.pallas import tpu as pltpu
from jax.sharding import Mesh
from jax.sharding import PartitionSpec as P

XY = ("x", "y")
ALL = ("x", "y", "z", "c")
F32 = jnp.float32
BF16 = jnp.bfloat16
LIMIT = 40 * 1024 * 1024
WIDE = 1024
SLOTS = 32
LANES = 256
MORE_SLOTS = 64
NT = (((1,), (1,)), ((), ()))
TN = (((0,), (0,)), ((), ()))


def _params():
    return pltpu.CompilerParams(vmem_limit_bytes=LIMIT)


def _cost(flops, moved):
    return pl.CostEstimate(flops=flops, bytes_accessed=moved, transcendentals=0)


def _row_ids(pos_ref, rows, tokens):
    at = lax.broadcasted_iota(jnp.int32, (2 * rows, tokens), 0)
    return jnp.where(at < rows, pos_ref[1] + at, pos_ref[2] + at - rows)


def _picks(hit, rank_ref, slots, first):
    slot = lax.broadcasted_iota(jnp.int32, (slots, rank_ref.shape[1]), 0) + first
    mine = jnp.where(slot == rank_ref[...], 1.0, 0.0).astype(BF16)
    hot = jnp.where(hit, 1.0, 0.0).astype(BF16)
    return lax.dot_general(mine, hot, NT, preferred_element_type=F32).astype(BF16)


def _thirds(v, count=3):
    rows = []
    for _ in range(count):
        rows.append(v.astype(BF16).astype(F32))
        v = v - rows[-1]
    return rows


def _forward_kernel(rows, pos_ref, tgt_ref, rank_ref, own_hbm, oth_hbm, *refs):
    pieces = refs[:-7]
    logit_ref, hid_hbm, part_hbm, tab, hid, part, sem = refs[-7:]
    tokens, width = hid.shape
    block = pieces[0].shape[0]
    z = pos_ref[0]
    copies = []
    for n, (turn, skip) in enumerate([(0, 0), (1, 0), (2, 0), (3, 0), (4, 0), (4, block // 2), (5, 0), (6, 0), (7, 0)]):
        at = pl.multiple_of(lax.rem(z + turn, 8) * block + skip, block // 2)
        copies.append(pltpu.make_async_copy(pieces[n], hid.at[pl.ds(at, pieces[n].shape[0])], sem.at[n]))
        copies[-1].start()
    n, loads = len(copies), []
    for i in range(width // WIDE):
        cut = pl.ds(i * WIDE, WIDE)
        for k, src in enumerate((own_hbm, oth_hbm)):
            loads.append(pltpu.make_async_copy(src.at[:, cut], tab.at[k, :, cut], sem.at[n]))
            loads[-1].start()
            n += 1
    for c in copies:
        c.wait()
    keep = pltpu.make_async_copy(hid, hid_hbm, sem.at[n])
    keep.start()
    for i in range(width // WIDE):
        cut = pl.ds(i * WIDE, WIDE)
        for k in range(2):
            loads[2 * i + k].wait()
        for k in range(2):
            a = lax.dot_general(tab[k, :, cut], hid[:, cut], NT, preferred_element_type=F32)
            if i == 0:
                logit_ref[pl.ds(k * rows, rows)] = a
            else:
                logit_ref[pl.ds(k * rows, rows)] += a
    logit = logit_ref[...]
    top = jnp.max(logit, axis=0, keepdims=True)
    raised = jnp.exp(logit - top)
    total = jnp.sum(raised, axis=0, keepdims=True)
    hit = _row_ids(pos_ref, rows, tokens) == tgt_ref[...]
    own = jnp.sum(jnp.where(hit, logit, 0.0), axis=0, keepdims=True)
    pick = _picks(hit, rank_ref, SLOTS, 0)
    lhs = jnp.concatenate([jnp.where(hit, 0.0, raised).T.astype(BF16), pick], axis=0)
    stats = jnp.concatenate(_thirds(top) + _thirds(total, 2) + _thirds(own), axis=0)
    feats = width // part.shape[0]
    outs = []
    for i in range(width // (2 * feats)):
        cut = pl.ds(2 * i * feats, 2 * feats)
        p = jnp.dot(lhs[:, :rows], tab[0, :, cut], preferred_element_type=F32)
        p += jnp.dot(lhs[:, rows:], tab[1, :, cut], preferred_element_type=F32)
        sums, q = p[:tokens].T.astype(BF16), p[tokens:]
        for k in range(2):
            part[2 * i + k, :feats] = sums[k * feats : (k + 1) * feats]
            mine = q[:, k * feats : (k + 1) * feats]
            tail = jnp.concatenate([mine[g * 8 : (g + 1) * 8, LANES:] for g in range(SLOTS // 8)], axis=1)
            part[2 * i + k, feats:] = jnp.concatenate([mine[:, :LANES], tail, stats], axis=0).astype(BF16)
        pair = pl.ds(2 * i, 2)
        outs.append(pltpu.make_async_copy(part.at[pair], part_hbm.at[pair], sem.at[n + 1 + i]))
        outs[-1].start()
    keep.wait()
    for c in outs:
        c.wait()


def _target_rows_kernel(rows, pos_ref, tgt_ref, rank_ref, own_ref, oth_ref, out_ref, pick):
    @pl.when(pl.program_id(0) == 0)
    def _():
        hit = _row_ids(pos_ref, rows, tgt_ref.shape[1]) == tgt_ref[...]
        pick[...] = _picks(hit, rank_ref, out_ref.shape[1], pos_ref[3])

    q = jnp.dot(pick[:, :rows], own_ref[...], preferred_element_type=F32)
    q += jnp.dot(pick[:, rows:], oth_ref[...], preferred_element_type=F32)
    feats = out_ref.shape[2]
    for k in range(out_ref.shape[0]):
        out_ref[k] = q[:, k * feats : (k + 1) * feats].astype(BF16)


def _combine_kernel(place_ref, more_ref, got, out_ref):
    peers, _, tokens = got.shape
    feats = more_ref.shape[0]
    place = place_ref[...]
    heads = jnp.concatenate([got[v, feats : feats + SLOTS] for v in range(peers)], axis=0)
    slot = lax.broadcasted_iota(jnp.int32, (peers * SLOTS, tokens), 0)
    hot = jnp.where(slot == place, 1.0, 0.0).astype(BF16)
    first = lax.dot_general(heads, hot, TN, preferred_element_type=F32)
    ends = [got[v, feats + SLOTS :].astype(F32) for v in range(peers)]
    tails = jnp.concatenate([e[:8] for e in ends], axis=0).astype(BF16)
    rest = feats - LANES
    eighth = lax.broadcasted_iota(jnp.int32, (peers * 8, tokens), 0)
    last = 0.0
    for g in range(SLOTS // 8):
        there = (eighth // 8) * SLOTS + g * 8 + eighth % 8
        hot_g = jnp.where(there == place, 1.0, 0.0).astype(BF16)
        last += lax.dot_general(tails[:, g * rest : (g + 1) * rest], hot_g, TN, preferred_element_type=F32)
    targets = jnp.concatenate([first, last], axis=0) + more_ref[...]
    tops = [e[8:9] + e[9:10] + e[10:11] for e in ends]
    top = functools.reduce(jnp.maximum, tops)
    total, hit, acc = 0.0, 0.0, 0.0
    for v in range(peers):
        scale = jnp.exp(tops[v] - top)
        total += (ends[v][11:12] + ends[v][12:13]) * scale
        hit += ends[v][13:14] + ends[v][14:15] + ends[v][15:16]
        acc += got[v, :feats].astype(F32) * scale
    both = jnp.concatenate([acc, targets], axis=0).T.astype(BF16)
    stats = jnp.concatenate(_thirds(top) + _thirds(total) + _thirds(hit) + [jnp.zeros((7, tokens), F32)], axis=0)
    stats = jnp.concatenate([stats, jnp.zeros((16, 2 * feats - tokens), F32)], axis=1).astype(BF16)
    n_tok = out_ref.shape[1] - 16
    for r in range(out_ref.shape[0]):
        out_ref[r, :n_tok] = both[r * n_tok : (r + 1) * n_tok]
        out_ref[r, n_tok:] = stats


def _finish_kernel(pos_ref, got, grad_ref, stat_ref, turned):
    peers, span, _ = got.shape
    n_tok, feats = grad_ref.shape
    tokens = stat_ref.shape[1]
    ends = [got[r, n_tok:, :tokens].astype(F32) for r in range(peers)]
    tops = [e[0:1] + e[1:2] + e[2:3] for e in ends]
    top = functools.reduce(jnp.maximum, tops)
    scales = [jnp.exp(t - top) for t in tops]
    total = sum((e[3:4] + e[4:5] + e[5:6]) * f for e, f in zip(ends, scales))
    hit = sum(e[6:7] + e[7:8] + e[8:9] for e in ends)
    stat_ref[...] = jnp.concatenate([top, total, hit, jnp.zeros((5, tokens), F32)], axis=0)
    inv = 1.0 / total
    rows = [f * inv for f in scales] + [jnp.exp(hit - top) * inv - 1.0, jnp.zeros((128 - peers - 1, tokens), F32)]
    turned[...] = jnp.concatenate(rows, axis=0).T
    own = turned[pl.ds(pl.multiple_of(pos_ref[0] * n_tok, n_tok), n_tok)]
    grad, targets = 0.0, 0.0
    for r in range(peers):
        block = got[r, :n_tok].astype(F32)
        grad += block[:, :feats] * own[:, r : r + 1]
        targets += block[:, feats:]
    grad_ref[...] = (grad + targets * own[:, peers : peers + 1]).astype(BF16)


def _grad_table_kernel(pos_ref, tok_ref, tgt_own, tgt_oth, stat_own, stat_oth, logit_own, logit_oth, h_own, h_oth, e_ref, out_ref, loss_ref, dl, hot):
    @pl.when(pl.program_id(0) == 0)
    def _():
        rows, tokens = logit_own.shape
        at = lax.broadcasted_iota(jnp.int32, hot.shape, 0) + pos_ref[1]
        hot[...] = jnp.where(at == tok_ref[...], 1.0, 0.0).astype(BF16)
        losses = []
        for k, (tgt, stat, logit) in enumerate(((tgt_own, stat_own, logit_own), (tgt_oth, stat_oth, logit_oth))):
            top, total = stat[0:1], stat[1:2]
            hit = jnp.where(at[:, :tokens] == tgt[...], 1.0, 0.0)
            dl[k] = (jnp.exp(logit[...] - top) * (1.0 / total) - hit).astype(BF16)
            losses.append(jnp.sum(top + jnp.log(total) - stat[2:3], keepdims=True))
        loss_ref[...] = losses[0] + losses[1]

    acc = jnp.dot(hot[...], e_ref[...], preferred_element_type=F32)
    acc += jnp.dot(dl[0], h_own[...], preferred_element_type=F32)
    acc += jnp.dot(dl[1], h_oth[...], preferred_element_type=F32)
    out_ref[...] = acc.astype(BF16)


def per_device(hidden, table, embed_grad, token_ids, target_ids):
    rows, width = table.shape
    n_tok = hidden.shape[0]
    nz, nxy = lax.axis_size("z"), lax.axis_size(XY)
    feats = width // nxy
    tokens = n_tok * nz
    xi, yi, zi, ci = (lax.axis_index(a) for a in ALL)
    chip = (xi * 4 + yi) * nz + zi
    swap = [(0, 1), (1, 0)]
    up = [(i, (i + 1) % nz) for i in range(nz)]
    down = [(i, (i - 1) % nz) for i in range(nz)]
    smem = pl.BlockSpec(memory_space=pltpu.SMEM)
    vmem = pl.BlockSpec(memory_space=pltpu.VMEM)
    hbm = pl.BlockSpec(memory_space=pl.ANY)

    def far_off(x):
        return pltpu.with_memory_space_constraint(x, pltpu.HBM)

    def pos_of(first):
        return jnp.stack([zi, (2 * chip + ci) * rows, (2 * chip + 1 - ci) * rows, first]).astype(jnp.int32)

    pos = pos_of(0)
    table_oth = lax.ppermute(table, "c", swap)
    ids = jnp.concatenate([target_ids, token_ids])
    ids = lax.all_to_all(jnp.broadcast_to(ids[None], (2 * nz, 2 * n_tok)), ("z", "c"), 0, 0, tiled=True)

    both = ids[:, :n_tok].reshape(nz, 2, n_tok).transpose(1, 0, 2).reshape(2, tokens)
    owner = both // (2 * rows)
    before = jnp.arange(tokens)[:, None] < jnp.arange(tokens)[None, :]
    ranks = jnp.sum((owner[:, :, None] == owner[:, None, :]) & before[None], axis=1).astype(jnp.int32)
    overflow = jnp.max(ranks) >= SLOTS
    targets = lax.dynamic_index_in_dim(both, ci, 0)
    targets_oth = lax.dynamic_index_in_dim(both, 1 - ci, 0)
    rank = lax.dynamic_index_in_dim(ranks, ci, 0)
    owner = targets // (2 * rows)
    here = owner % nz == zi
    place = jnp.where(here & (rank < SLOTS), owner // nz * SLOTS + rank, -1)
    toks = ids[:, n_tok:].reshape(1, 2 * tokens)

    def round_of(first):
        width_q = 2 * feats
        row = pl.BlockSpec((1, tokens), lambda i: (0, 0))
        sent = pl.pallas_call(
            functools.partial(_target_rows_kernel, rows),
            grid=(width // width_q,),
            in_specs=[smem, row, row, *[pl.BlockSpec((rows, width_q), lambda i: (0, i))] * 2],
            out_specs=pl.BlockSpec((2, MORE_SLOTS, feats), lambda i: (i, 0, 0)),
            out_shape=jax.ShapeDtypeStruct((nxy, MORE_SLOTS, feats), BF16),
            scratch_shapes=[pltpu.VMEM((MORE_SLOTS, 2 * rows), BF16)],
            compiler_params=_params(),
            cost_estimate=_cost(4 * rows * MORE_SLOTS * width, 4 * rows * width),
            name="target_rows",
        )(pos_of(first), targets, rank, table, table_oth)
        got = lax.all_to_all(sent, XY, 0, 0, tiled=True).reshape(nxy * MORE_SLOTS, feats)
        inside = here & (rank >= first) & (rank < first + MORE_SLOTS)
        slot = jnp.where(inside, owner // nz * MORE_SLOTS + rank - first, -1)
        hot = (jnp.arange(nxy * MORE_SLOTS, dtype=jnp.int32)[:, None] == slot).astype(BF16)
        return lax.dot_general(got, hot, TN, preferred_element_type=F32)

    def more():
        return sum(round_of(first) for first in range(SLOTS, tokens, MORE_SLOTS))

    u, d = lax.optimization_barrier((lax.ppermute(hidden, "z", up), lax.ppermute(hidden, "z", down)))
    ups, downs = [u], [d]
    u, d, place, rank, targets, targets_oth, toks = lax.optimization_barrier(
        (lax.ppermute(u, "z", up), lax.ppermute(d, "z", down), place, rank, targets, targets_oth, toks)
    )
    ups.append(u)
    downs.append(d)
    u, d = lax.optimization_barrier((lax.ppermute(u, "z", up), lax.ppermute(d, "z", down)))
    ups.append(u)
    downs.append(d)
    half = n_tok // 2
    q_more = lax.cond(overflow, more, lambda: jnp.zeros((feats, tokens), F32))
    *far, q_more = lax.optimization_barrier((lax.ppermute(u[:half], "z", up), lax.ppermute(d[half:], "z", down), q_more))
    pieces = [hidden, *downs, *far, *ups[::-1]]

    span = feats + SLOTS + 16
    logit, h_own, part = pl.pallas_call(
        functools.partial(_forward_kernel, rows),
        in_specs=[smem, vmem, vmem] + [hbm] * (2 + len(pieces)),
        out_specs=[vmem, hbm, hbm],
        out_shape=[
            jax.ShapeDtypeStruct((2 * rows, tokens), F32),
            pltpu.HBM((tokens, width), BF16),
            pltpu.HBM((nxy, span, tokens), BF16),
        ],
        scratch_shapes=[
            pltpu.VMEM((2, rows, width), BF16),
            pltpu.VMEM((tokens, width), BF16),
            pltpu.VMEM((nxy, span, tokens), BF16),
            pltpu.SemaphoreType.DMA((len(pieces) + 2 * (width // WIDE) + 1 + nxy // 2,)),
        ],
        compiler_params=_params(),
        cost_estimate=_cost(8 * rows * tokens * width, 4 * rows * width + 6 * tokens * width),
        name="forward",
    )(pos, targets, rank, table, table_oth, *pieces)

    e_src, _ = lax.optimization_barrier((embed_grad, far[0]))
    e_all = lax.all_gather(e_src, ("z", "c"), axis=0, tiled=True)

    got = lax.all_to_all(part, XY, 0, 0, tiled=True)
    h_oth = lax.ppermute(h_own, "c", swap)
    logit_oth = lax.ppermute(logit[rows:], "c", swap)

    by_z = pl.pallas_call(
        _combine_kernel,
        in_specs=[vmem] * 3,
        out_specs=vmem,
        out_shape=jax.ShapeDtypeStruct((nz, n_tok + 16, 2 * feats), BF16),
        compiler_params=_params(),
        cost_estimate=_cost(10**6, 10**5),
        name="combine",
    )(place, q_more, got)
    by_z = lax.all_to_all(by_z, "z", 0, 0, tiled=True)

    grad_hidden, stat = pl.pallas_call(
        _finish_kernel,
        in_specs=[smem, vmem],
        out_specs=[vmem, vmem],
        out_shape=[jax.ShapeDtypeStruct((n_tok, feats), BF16), jax.ShapeDtypeStruct((8, tokens), F32)],
        scratch_shapes=[pltpu.VMEM((tokens, 128), F32)],
        compiler_params=_params(),
        cost_estimate=_cost(10**6, 10**5),
        name="finish",
    )(pos, by_z)
    stat_oth = lax.ppermute(stat, "c", swap)

    whole = lambda *shape: pl.BlockSpec(shape, lambda i: (0,) * len(shape))
    col = lambda n: pl.BlockSpec((n, WIDE), lambda i: (0, i))
    grad_table, loss = pl.pallas_call(
        _grad_table_kernel,
        grid=(width // WIDE,),
        in_specs=[smem, whole(1, 2 * tokens), *[whole(1, tokens)] * 2, *[whole(8, tokens)] * 2, *[whole(rows, tokens)] * 2]
        + [col(tokens), col(tokens), col(2 * tokens)],
        out_specs=[col(rows), whole(1, 1)],
        out_shape=[jax.ShapeDtypeStruct((rows, width), BF16), jax.ShapeDtypeStruct((1, 1), F32)],
        scratch_shapes=[pltpu.VMEM((2, rows, tokens), BF16), pltpu.VMEM((rows, 2 * tokens), BF16)],
        compiler_params=_params(),
        cost_estimate=_cost(8 * rows * tokens * width, 8 * tokens * width + 2 * rows * width),
        name="grad_table",
    )(pos, toks, targets, targets_oth, stat, stat_oth, *map(far_off, (logit, logit_oth, h_own, h_oth, e_all)))
    return grad_hidden, grad_table, loss[0, 0]


def solution(mesh):
    fine = Mesh(mesh.devices.reshape(4, 4, 8, 2), ALL)
    in_specs = (P(("z", "c"), None), P(ALL, None), P(("z", "c"), None), P(("z", "c")), P(("z", "c")))
    out_specs = (P(("z", "c"), XY), P(ALL, None), P())
    return jax.shard_map(per_device, mesh=fine, in_specs=in_specs, out_specs=out_specs, check_vma=False)
```

```python
import functools

import jax
import jax.numpy as jnp
from jax import lax
from jax.experimental import pallas as pl
from jax.experimental.pallas import tpu as pltpu
from jax.sharding import Mesh
from jax.sharding import PartitionSpec as P

XY = ("x", "y")
ALL = ("x", "y", "z", "c")
F32 = jnp.float32
BF16 = jnp.bfloat16
LIMIT = 40 * 1024 * 1024
WIDE = 1024
SLOTS = 8
LANES = 128
MORE_SLOTS = 64
NT = (((1,), (1,)), ((), ()))
TN = (((0,), (0,)), ((), ()))


def _params():
    return pltpu.CompilerParams(vmem_limit_bytes=LIMIT)


def _cost(flops, moved):
    return pl.CostEstimate(flops=flops, bytes_accessed=moved, transcendentals=0)


def _row_ids(pos_ref, rows, tokens):
    at = lax.broadcasted_iota(jnp.int32, (2 * rows, tokens), 0)
    return jnp.where(at < rows, pos_ref[1] + at, pos_ref[2] + at - rows)


def _picks(hit, rank_ref, slots, first):
    slot = lax.broadcasted_iota(jnp.int32, (slots, rank_ref.shape[1]), 0) + first
    mine = jnp.where(slot == rank_ref[...], 1.0, 0.0).astype(BF16)
    hot = jnp.where(hit, 1.0, 0.0).astype(BF16)
    return jnp.minimum(lax.dot_general(mine, hot, NT, preferred_element_type=F32), 1.0).astype(BF16)


def _thirds(v, count=3):
    rows = []
    for _ in range(count):
        rows.append(v.astype(BF16).astype(F32))
        v = v - rows[-1]
    return rows


def _forward_kernel(rows, pos_ref, tgt_ref, rank_ref, own_hbm, oth_hbm, *refs):
    pieces = refs[:-8]
    logit_hbm, hid_hbm, part_hbm, logit_ref, tab, hid, part, sem = refs[-8:]
    tokens, width = hid.shape
    copies, at = [], 0
    for n, p in enumerate(pieces):
        copies.append(pltpu.make_async_copy(p, hid.at[pl.ds(at, p.shape[0])], sem.at[n]))
        copies[-1].start()
        at += p.shape[0]
    n, loads = len(copies), []
    for i in range(width // WIDE):
        cut = pl.ds(i * WIDE, WIDE)
        for k, src in enumerate((own_hbm, oth_hbm)):
            loads.append(pltpu.make_async_copy(src.at[:, cut], tab.at[k, :, cut], sem.at[n]))
            loads[-1].start()
            n += 1
    for c in copies:
        c.wait()
    keep = pltpu.make_async_copy(hid, hid_hbm, sem.at[n])
    keep.start()
    for i in range(width // WIDE):
        cut = pl.ds(i * WIDE, WIDE)
        for k in range(2):
            loads[2 * i + k].wait()
        for k in range(2):
            a = lax.dot_general(tab[k, :, cut], hid[:, cut], NT, preferred_element_type=F32)
            if i == 0:
                logit_ref[pl.ds(k * rows, rows)] = a
            else:
                logit_ref[pl.ds(k * rows, rows)] += a
    held = pltpu.make_async_copy(logit_ref, logit_hbm, sem.at[n + 1])
    held.start()
    logit = logit_ref[...]
    top = jnp.max(logit, axis=0, keepdims=True)
    raised = jnp.exp(logit - top)
    total = jnp.sum(raised, axis=0, keepdims=True)
    hit = _row_ids(pos_ref, rows, tokens) == tgt_ref[...]
    own = jnp.sum(jnp.where(hit, logit, 0.0), axis=0, keepdims=True)
    pick = _picks(hit, rank_ref, SLOTS, 0)
    lhs = jnp.concatenate([jnp.where(hit, 0.0, raised).T.astype(BF16), pick], axis=0)
    stats = jnp.concatenate(_thirds(top) + _thirds(total, 2) + _thirds(own), axis=0)
    feats = width // part.shape[0]
    outs = []
    for i in range(width // (2 * feats)):
        cut = pl.ds(2 * i * feats, 2 * feats)
        p = jnp.dot(lhs[:, :rows], tab[0, :, cut], preferred_element_type=F32)
        p += jnp.dot(lhs[:, rows:], tab[1, :, cut], preferred_element_type=F32)
        sums, q = p[:tokens].T.astype(BF16), p[tokens:]
        for k in range(2):
            part[2 * i + k, :feats] = sums[k * feats : (k + 1) * feats]
            mine = q[:, k * feats : (k + 1) * feats]
            last = jnp.concatenate([mine[:, 2 * LANES :], jnp.zeros((SLOTS, 3 * LANES - feats), F32)], axis=1)
            part[2 * i + k, feats:] = jnp.concatenate([mine[:, :LANES], mine[:, LANES : 2 * LANES], last, stats], axis=0).astype(BF16)
        pair = pl.ds(2 * i, 2)
        outs.append(pltpu.make_async_copy(part.at[pair], part_hbm.at[pair], sem.at[n + 2 + i]))
        outs[-1].start()
    keep.wait()
    held.wait()
    for c in outs:
        c.wait()


def _target_rows_kernel(rows, pos_ref, tgt_ref, rank_ref, own_ref, oth_ref, out_ref, pick):
    @pl.when(pl.program_id(0) == 0)
    def _():
        hit = _row_ids(pos_ref, rows, tgt_ref.shape[1]) == tgt_ref[...]
        pick[...] = _picks(hit, rank_ref, out_ref.shape[1], pos_ref[3])

    q = jnp.dot(pick[:, :rows], own_ref[...], preferred_element_type=F32)
    q += jnp.dot(pick[:, rows:], oth_ref[...], preferred_element_type=F32)
    feats = out_ref.shape[2]
    for k in range(out_ref.shape[0]):
        out_ref[k] = q[:, k * feats : (k + 1) * feats].astype(BF16)


def _summed(place, got, feats):
    peers, _, tokens = got.shape
    slot = lax.broadcasted_iota(jnp.int32, (peers * SLOTS, tokens), 0)
    hot = jnp.where(slot == place, 1.0, 0.0).astype(BF16)
    ends = [got[v, feats:].astype(F32) for v in range(peers)]
    targets = []
    for k in range(3):
        slots = jnp.concatenate([e[k * SLOTS : (k + 1) * SLOTS] for e in ends], axis=0).astype(BF16)
        targets.append(lax.dot_general(slots, hot, TN, preferred_element_type=F32))
    targets = jnp.concatenate(targets, axis=0)[:feats]
    ends = [e[3 * SLOTS :] for e in ends]
    tops = [e[0:1] + e[1:2] + e[2:3] for e in ends]
    top = functools.reduce(jnp.maximum, tops)
    total, hit, acc = 0.0, 0.0, 0.0
    for v in range(peers):
        scale = jnp.exp(tops[v] - top)
        total += (ends[v][3:4] + ends[v][4:5]) * scale
        hit += ends[v][5:6] + ends[v][6:7] + ends[v][7:8]
        acc += got[v, :feats].astype(F32) * scale
    return acc, targets, top, total, hit


def _combine_kernel(pos_ref, place_a, place_b, more_ref, got_a, got_b, out_ref):
    feats, tokens = more_ref.shape
    z = pos_ref[0]
    a, b = _summed(place_a[...], got_a, feats), _summed(place_b[...], got_b, feats)
    acc, targets, top, total, hit = (jnp.concatenate(v, axis=1) for v in zip(a, b))
    both = jnp.concatenate([acc, targets + more_ref[...]], axis=0).T.astype(BF16)
    peers, n_tok = out_ref.shape[0], out_ref.shape[1] - 8
    stats = jnp.concatenate(_thirds(top) + _thirds(total) + _thirds(hit) + [jnp.zeros((7, tokens), F32)], axis=0)
    stats = pltpu.roll(stats, lax.rem(z + peers - 1, peers) * n_tok, 1)
    pairs = [jnp.concatenate([stats[2 * k : 2 * k + 1], stats[2 * k + 1 : 2 * k + 2]], axis=1) for k in range(8)]
    stats = jnp.concatenate(pairs, axis=0)
    stats = jnp.concatenate([stats, jnp.zeros((8, 2 * feats - 2 * tokens), F32)], axis=1).astype(BF16)
    for p in range(peers):
        out_ref[lax.rem(z + p + peers - 1, peers), :n_tok] = both[p * n_tok : (p + 1) * n_tok]
        out_ref[p, n_tok:] = stats


def _finish_kernel(pos_ref, got, grad_ref, stat_ref, turned):
    peers, span, _ = got.shape
    n_tok, feats = grad_ref.shape
    tokens = stat_ref.shape[1]
    wide = [got[r, n_tok:, : 2 * tokens].astype(F32) for r in range(peers)]
    ends = [[w[k // 2 : k // 2 + 1, k % 2 * tokens : (k % 2 + 1) * tokens] for k in range(9)] for w in wide]
    tops = [e[0] + e[1] + e[2] for e in ends]
    top = functools.reduce(jnp.maximum, tops)
    scales = [jnp.exp(t - top) for t in tops]
    total = sum((e[3] + e[4] + e[5]) * f for e, f in zip(ends, scales))
    hit = sum(e[6] + e[7] + e[8] for e in ends)
    stat_ref[...] = jnp.concatenate([top, total, hit, jnp.zeros((5, tokens), F32)], axis=0)
    inv = 1.0 / total
    rows = [f * inv for f in scales] + [jnp.exp(hit - top) * inv - 1.0, jnp.zeros((128 - peers - 1, tokens), F32)]
    turned[...] = jnp.concatenate(rows, axis=0).T
    own = turned[pl.ds(pl.multiple_of(pos_ref[0] * n_tok, n_tok), n_tok)]
    grad, targets = 0.0, 0.0
    for r in range(peers):
        block = got[r, :n_tok].astype(F32)
        grad += block[:, :feats] * own[:, r : r + 1]
        targets += block[:, feats:]
    grad_ref[...] = (grad + targets * own[:, peers : peers + 1]).astype(BF16)


def _grad_table_kernel(pos_ref, tok_ref, tgt_own, tgt_oth, stat_own, stat_oth, *refs):
    own_a, own_b, oth_a, oth_b, h_own_a, h_own_b, h_oth_a, h_oth_b, e_ref, out_ref, loss_ref, dl, hot = refs

    @pl.when(pl.program_id(0) == 0)
    def _():
        rows, tokens = own_a.shape[0], tgt_own.shape[1]
        at = lax.broadcasted_iota(jnp.int32, hot.shape, 0) + pos_ref[1]
        hot[...] = jnp.where(at == tok_ref[...], 1.0, 0.0).astype(BF16)
        turn = lax.rem(9 - pos_ref[0], 8) * (tokens // 8)
        losses = []
        for k, (tgt, stat, a, b) in enumerate(((tgt_own, stat_own, own_a, own_b), (tgt_oth, stat_oth, oth_a, oth_b))):
            losses.append(jnp.sum(stat[0:1] + jnp.log(stat[1:2]) - stat[2:3], keepdims=True))
            turned = pltpu.roll(stat[...], turn, 1)
            hit = jnp.where(at[:, :tokens] == tgt[...], 1.0, 0.0)
            logit = jnp.concatenate([a[...], b[...]], axis=1)
            dl[k] = (jnp.exp(logit - turned[0:1]) * (1.0 / turned[1:2]) - hit).astype(BF16)
        loss_ref[...] = losses[0] + losses[1]

    acc = jnp.dot(hot[...], e_ref[...], preferred_element_type=F32)
    acc += jnp.dot(dl[0], jnp.concatenate([h_own_a[...], h_own_b[...]], axis=0), preferred_element_type=F32)
    acc += jnp.dot(dl[1], jnp.concatenate([h_oth_a[...], h_oth_b[...]], axis=0), preferred_element_type=F32)
    out_ref[...] = acc.astype(BF16)


def per_device(hidden, table, embed_grad, token_ids, target_ids):
    rows, width = table.shape
    n_tok = hidden.shape[0]
    nz, nxy = lax.axis_size("z"), lax.axis_size(XY)
    feats = width // nxy
    tokens = n_tok * nz
    xi, yi, zi, ci = (lax.axis_index(a) for a in ALL)
    chip = (xi * 4 + yi) * nz + zi
    swap = [(0, 1), (1, 0)]
    up = [(i, (i + 1) % nz) for i in range(nz)]
    down = [(i, (i - 1) % nz) for i in range(nz)]
    smem = pl.BlockSpec(memory_space=pltpu.SMEM)
    vmem = pl.BlockSpec(memory_space=pltpu.VMEM)
    hbm = pl.BlockSpec(memory_space=pl.ANY)

    def far_off(x):
        return pltpu.with_memory_space_constraint(x, pltpu.HBM)

    def pos_of(first):
        return jnp.stack([zi, (2 * chip + ci) * rows, (2 * chip + 1 - ci) * rows, first]).astype(jnp.int32)

    pos = pos_of(0)
    table_oth = lax.ppermute(table, "c", swap)
    ids = jnp.concatenate([target_ids, token_ids])
    ids = lax.all_to_all(jnp.broadcast_to(ids[None], (2 * nz, 2 * n_tok)), ("z", "c"), 0, 0, tiled=True)

    u, d = lax.optimization_barrier((lax.ppermute(hidden, "z", up), lax.ppermute(hidden, "z", down)))
    ups, downs = [u], [d]
    u, d, ids = lax.optimization_barrier((lax.ppermute(u, "z", up), lax.ppermute(d, "z", down), ids))
    ups.append(u)
    downs.append(d)

    both = ids[:, :n_tok].reshape(nz, 2, n_tok).transpose(1, 0, 2)
    both = jnp.roll(both, 1 - zi, axis=1).reshape(2, tokens)
    part_of = jnp.arange(tokens) // (tokens // 2)
    alike = part_of[:, None] == part_of[None, :]
    before = jnp.arange(tokens)[:, None] < jnp.arange(tokens)[None, :]
    same = both[:, :, None] == both[:, None, :]
    fresh = ~jnp.any(same & (alike & before)[None], axis=1)
    owner = both // (2 * rows)
    below = (owner[:, :, None] == owner[:, None, :]) & (both[:, :, None] < both[:, None, :]) & alike[None] & fresh[:, :, None]
    ranks = jnp.sum(below, axis=1).astype(jnp.int32)
    overflow = jnp.max(ranks) >= SLOTS
    targets = lax.dynamic_index_in_dim(both, ci, 0)
    targets_oth = lax.dynamic_index_in_dim(both, 1 - ci, 0)
    rank = lax.dynamic_index_in_dim(ranks, ci, 0)
    owner = targets // (2 * rows)
    here = owner % nz == zi
    place = jnp.where(here & (rank < SLOTS), owner // nz * SLOTS + rank, -1)
    toks = ids[:, n_tok:].reshape(1, 2 * tokens)

    def round_of(first, part):
        rank_in = jnp.where(part_of[None] == part, rank, -1)
        width_q = 2 * feats
        row = pl.BlockSpec((1, tokens), lambda i: (0, 0))
        sent = pl.pallas_call(
            functools.partial(_target_rows_kernel, rows),
            grid=(width // width_q,),
            in_specs=[smem, row, row, *[pl.BlockSpec((rows, width_q), lambda i: (0, i))] * 2],
            out_specs=pl.BlockSpec((2, MORE_SLOTS, feats), lambda i: (i, 0, 0)),
            out_shape=jax.ShapeDtypeStruct((nxy, MORE_SLOTS, feats), BF16),
            scratch_shapes=[pltpu.VMEM((MORE_SLOTS, 2 * rows), BF16)],
            compiler_params=_params(),
            cost_estimate=_cost(4 * rows * MORE_SLOTS * width, 4 * rows * width),
            name="target_rows",
        )(pos_of(first), targets, rank_in, table, table_oth)
        got = lax.all_to_all(sent, XY, 0, 0, tiled=True).reshape(nxy * MORE_SLOTS, feats)
        inside = here & (rank_in >= first) & (rank_in < first + MORE_SLOTS)
        slot = jnp.where(inside, owner // nz * MORE_SLOTS + rank_in - first, -1)
        hot = (jnp.arange(nxy * MORE_SLOTS, dtype=jnp.int32)[:, None] == slot).astype(BF16)
        return lax.dot_general(got, hot, TN, preferred_element_type=F32)

    def more():
        return sum(round_of(first, part) for part in range(2) for first in range(SLOTS, tokens // 2, MORE_SLOTS))

    span = feats + 3 * SLOTS + 8
    wide = tokens // 2

    def forward(name, part, share, *pieces):
        cut = slice(part * wide, (part + 1) * wide)
        return pl.pallas_call(
            functools.partial(_forward_kernel, rows),
            in_specs=[smem, vmem, vmem] + [hbm] * (2 + len(pieces)),
            out_specs=[hbm] * 3,
            out_shape=[
                pltpu.HBM((2 * rows, wide), F32),
                pltpu.HBM((wide, width), BF16),
                pltpu.HBM((nxy, span, wide), BF16),
            ],
            scratch_shapes=[
                pltpu.VMEM((2 * rows, wide), F32),
                pltpu.VMEM((2, rows, width), BF16),
                pltpu.VMEM((wide, width), BF16),
                pltpu.VMEM((nxy, span, wide), BF16),
                pltpu.SemaphoreType.DMA((len(pieces) + 2 * (width // WIDE) + 2 + nxy // 2,)),
            ],
            compiler_params=_params(),
            cost_estimate=_cost(8 * rows * wide * width // share, (4 * rows * width + 6 * wide * width) // share),
            name=name,
        )(pos, targets[:, cut], rank[:, cut], table, table_oth, *pieces)

    half = n_tok // 2
    u2, d2 = u, d
    u, d = lax.ppermute(u2, "z", up), lax.ppermute(d2, "z", down)
    far = (
        lax.ppermute(u2[:half], "z", [(i, (i + 2) % nz) for i in range(nz)]),
        lax.ppermute(d2[half:], "z", [(i, (i - 2) % nz) for i in range(nz)]),
    )
    logit_a, h_own_a, part_a = forward("forward_a", 0, 1, ups[0], far_off(hidden), downs[0], downs[1])
    q_more = lax.cond(overflow, more, lambda: jnp.zeros((feats, tokens), F32))
    u, d, *far, part_a, q_more = lax.optimization_barrier((u, d, *far, part_a, q_more))
    got_a = lax.all_to_all(part_a, XY, 0, 0, tiled=True)
    logit_b, h_own_b, part_b = forward("forward_b", 1, 1, d, *far, u, ups[1])
    got_b = lax.all_to_all(part_b, XY, 0, 0, tiled=True)

    e_src, _ = lax.optimization_barrier((embed_grad, far[0]))
    e_all = lax.all_gather(e_src, ("z", "c"), axis=0, tiled=True)

    h_oth_a, h_oth_b, oth_a, oth_b = (
        lax.ppermute(v, "c", swap) for v in (h_own_a, h_own_b, logit_a[rows:], logit_b[rows:])
    )
    place_a, place_b = place[:, :wide], place[:, wide:]

    by_z = pl.pallas_call(
        _combine_kernel,
        in_specs=[smem] + [vmem] * 5,
        out_specs=vmem,
        out_shape=jax.ShapeDtypeStruct((nz, n_tok + 8, 2 * feats), BF16),
        compiler_params=_params(),
        cost_estimate=_cost(10**6, 10**5),
        name="combine",
    )(pos, place_a, place_b, q_more, got_a, got_b)
    by_z = lax.all_to_all(by_z, "z", 0, 0, tiled=True)

    grad_hidden, stat = pl.pallas_call(
        _finish_kernel,
        in_specs=[smem, vmem],
        out_specs=[vmem, vmem],
        out_shape=[jax.ShapeDtypeStruct((n_tok, feats), BF16), jax.ShapeDtypeStruct((8, tokens), F32)],
        scratch_shapes=[pltpu.VMEM((tokens, 128), F32)],
        compiler_params=_params(),
        cost_estimate=_cost(10**6, 10**5),
        name="finish",
    )(pos, by_z)
    stat_oth = lax.ppermute(stat, "c", swap)

    whole = lambda *shape: pl.BlockSpec(shape, lambda i: (0,) * len(shape))
    col = lambda n: pl.BlockSpec((n, WIDE), lambda i: (0, i))
    grad_table, loss = pl.pallas_call(
        _grad_table_kernel,
        grid=(width // WIDE,),
        in_specs=[smem, whole(1, 2 * tokens), *[whole(1, tokens)] * 2, *[whole(8, tokens)] * 2, *[whole(rows, wide)] * 4]
        + [col(wide)] * 4
        + [col(2 * tokens)],
        out_specs=[col(rows), whole(1, 1)],
        out_shape=[jax.ShapeDtypeStruct((rows, width), BF16), jax.ShapeDtypeStruct((1, 1), F32)],
        scratch_shapes=[pltpu.VMEM((2, rows, tokens), BF16), pltpu.VMEM((rows, 2 * tokens), BF16)],
        compiler_params=_params(),
        cost_estimate=_cost(8 * rows * tokens * width, 8 * tokens * width + 2 * rows * width),
        name="grad_table",
    )(pos, toks, targets, targets_oth, stat, stat_oth, logit_a, logit_b, oth_a, oth_b, *map(far_off, (h_own_a, h_own_b, h_oth_a, h_oth_b, e_all)))
    return grad_hidden, grad_table, loss[0, 0]


def solution(mesh):
    fine = Mesh(mesh.devices.reshape(4, 4, 8, 2), ALL)
    in_specs = (P(("z", "c"), None), P(ALL, None), P(("z", "c"), None), P(("z", "c")), P(("z", "c")))
    out_specs = (P(("z", "c"), XY), P(ALL, None), P())
    return jax.shard_map(per_device, mesh=fine, in_specs=in_specs, out_specs=out_specs, check_vma=False)
```

```python
import functools

import jax
import jax.numpy as jnp
from jax import lax
from jax.experimental import pallas as pl
from jax.experimental.pallas import tpu as pltpu
from jax.sharding import Mesh
from jax.sharding import PartitionSpec as P

XY = ("x", "y")
ALL = ("x", "y", "z", "c")
F32 = jnp.float32
BF16 = jnp.bfloat16
LIMIT = 40 * 1024 * 1024
WIDE = 1024
TABLE_WIDE = 1280
SLOTS = 8
LANES = 128
MORE_SLOTS = 64
NT = (((1,), (1,)), ((), ()))
TN = (((0,), (0,)), ((), ()))


def _params():
    return pltpu.CompilerParams(vmem_limit_bytes=LIMIT)


def _cost(flops, moved):
    return pl.CostEstimate(flops=flops, bytes_accessed=moved, transcendentals=0)


def _row_ids(pos_ref, rows, tokens):
    at = lax.broadcasted_iota(jnp.int32, (2 * rows, tokens), 0)
    return jnp.where(at < rows, pos_ref[1] + at, pos_ref[2] + at - rows)


def _picks(hit, rank_ref, slots, first):
    slot = lax.broadcasted_iota(jnp.int32, (slots, rank_ref.shape[1]), 0) + first
    mine = jnp.where(slot == rank_ref[...], 1.0, 0.0).astype(BF16)
    hot = jnp.where(hit, 1.0, 0.0).astype(BF16)
    return jnp.minimum(lax.dot_general(mine, hot, NT, preferred_element_type=F32), 1.0).astype(BF16)


def _thirds(v, count=3):
    rows = []
    for _ in range(count):
        rows.append(v.astype(BF16).astype(F32))
        v = v - rows[-1]
    return rows


def _forward_kernel(rows, pos_ref, tgt_ref, rank_ref, own_hbm, oth_hbm, *refs):
    pieces = refs[:-8]
    logit_hbm, hid_hbm, part_hbm, logit_ref, tab, hid, part, sem = refs[-8:]
    tokens, width = hid.shape
    copies, at = [], 0
    for n, p in enumerate(pieces):
        copies.append(pltpu.make_async_copy(p, hid.at[pl.ds(at, p.shape[0])], sem.at[n]))
        copies[-1].start()
        at += p.shape[0]
    n, loads = len(copies), []
    for i in range(width // WIDE):
        cut = pl.ds(i * WIDE, WIDE)
        for k, src in enumerate((own_hbm, oth_hbm)):
            loads.append(pltpu.make_async_copy(src.at[:, cut], tab.at[k, :, cut], sem.at[n]))
            loads[-1].start()
            n += 1
    for c in copies:
        c.wait()
    keep = pltpu.make_async_copy(hid, hid_hbm, sem.at[n])
    keep.start()
    for i in range(width // WIDE):
        cut = pl.ds(i * WIDE, WIDE)
        for k in range(2):
            loads[2 * i + k].wait()
        for k in range(2):
            a = lax.dot_general(tab[k, :, cut], hid[:, cut], NT, preferred_element_type=F32)
            if i == 0:
                logit_ref[pl.ds(k * rows, rows)] = a
            else:
                logit_ref[pl.ds(k * rows, rows)] += a
    held = pltpu.make_async_copy(logit_ref, logit_hbm, sem.at[n + 1])
    held.start()
    logit = logit_ref[...]
    top = jnp.max(logit, axis=0, keepdims=True)
    raised = jnp.exp(logit - top)
    total = jnp.sum(raised, axis=0, keepdims=True)
    hit = _row_ids(pos_ref, rows, tokens) == tgt_ref[...]
    own = jnp.sum(jnp.where(hit, logit, 0.0), axis=0, keepdims=True)
    pick = _picks(hit, rank_ref, SLOTS, 0)
    lhs = jnp.concatenate([jnp.where(hit, 0.0, raised).T.astype(BF16), pick], axis=0)
    stats = jnp.concatenate(_thirds(top) + _thirds(total, 2) + _thirds(own), axis=0)
    feats = width // part.shape[0]
    outs = []
    for i in range(width // (2 * feats)):
        cut = pl.ds(2 * i * feats, 2 * feats)
        p = jnp.dot(lhs[:, :rows], tab[0, :, cut], preferred_element_type=F32)
        p += jnp.dot(lhs[:, rows:], tab[1, :, cut], preferred_element_type=F32)
        sums, q = p[:tokens].T.astype(BF16), p[tokens:]
        for k in range(2):
            part[2 * i + k, :feats] = sums[k * feats : (k + 1) * feats]
            mine = q[:, k * feats : (k + 1) * feats]
            last = jnp.concatenate([mine[:, 2 * LANES :], jnp.zeros((SLOTS, 3 * LANES - feats), F32)], axis=1)
            part[2 * i + k, feats:] = jnp.concatenate([mine[:, :LANES], mine[:, LANES : 2 * LANES], last, stats], axis=0).astype(BF16)
        pair = pl.ds(2 * i, 2)
        outs.append(pltpu.make_async_copy(part.at[pair], part_hbm.at[pair], sem.at[n + 2 + i]))
        outs[-1].start()
    keep.wait()
    held.wait()
    for c in outs:
        c.wait()


def _target_rows_kernel(rows, pos_ref, tgt_ref, rank_ref, own_ref, oth_ref, out_ref, pick):
    @pl.when(pl.program_id(0) == 0)
    def _():
        hit = _row_ids(pos_ref, rows, tgt_ref.shape[1]) == tgt_ref[...]
        pick[...] = _picks(hit, rank_ref, out_ref.shape[1], pos_ref[3])

    q = jnp.dot(pick[:, :rows], own_ref[...], preferred_element_type=F32)
    q += jnp.dot(pick[:, rows:], oth_ref[...], preferred_element_type=F32)
    feats = out_ref.shape[2]
    for k in range(out_ref.shape[0]):
        out_ref[k] = q[:, k * feats : (k + 1) * feats].astype(BF16)


def _summed(place, got, feats):
    peers, _, tokens = got.shape
    slot = lax.broadcasted_iota(jnp.int32, (peers * SLOTS, tokens), 0)
    hot = jnp.where(slot == place, 1.0, 0.0).astype(BF16)
    ends = [got[v, feats:].astype(F32) for v in range(peers)]
    targets = []
    for k in range(3):
        slots = jnp.concatenate([e[k * SLOTS : (k + 1) * SLOTS] for e in ends], axis=0).astype(BF16)
        targets.append(lax.dot_general(slots, hot, TN, preferred_element_type=F32))
    targets = jnp.concatenate(targets, axis=0)[:feats]
    ends = [e[3 * SLOTS :] for e in ends]
    tops = [e[0:1] + e[1:2] + e[2:3] for e in ends]
    top = functools.reduce(jnp.maximum, tops)
    total, hit, acc = 0.0, 0.0, 0.0
    for v in range(peers):
        scale = jnp.exp(tops[v] - top)
        total += (ends[v][3:4] + ends[v][4:5]) * scale
        hit += ends[v][5:6] + ends[v][6:7] + ends[v][7:8]
        acc += got[v, :feats].astype(F32) * scale
    return acc, targets, top, total, hit


def _half_kernel(place_ref, got_ref, sums_ref, stat_ref):
    acc, targets, top, total, hit = _summed(place_ref[...], got_ref, sums_ref.shape[1] // 2)
    sums_ref[...] = jnp.concatenate([acc, targets], axis=0).T.astype(BF16)
    stat_ref[...] = jnp.concatenate([top, total, hit, jnp.zeros((5, top.shape[1]), F32)], axis=0)


def _combine_kernel(pos_ref, place_ref, more_ref, got_ref, first_ref, stat_ref, out_ref):
    z = pos_ref[0]
    acc, targets, *rows = _summed(place_ref[...], got_ref, more_ref.shape[0])
    rest = jnp.concatenate([acc, targets], axis=0).T.astype(BF16)
    both = jnp.concatenate([first_ref[...], rest], axis=0)
    feats, tokens = acc.shape[0], both.shape[0]
    both = both + jnp.concatenate([jnp.zeros((feats, tokens), F32), more_ref[...]], axis=0).T.astype(BF16)
    top, total, hit = (jnp.concatenate([stat_ref[k : k + 1], v], axis=1) for k, v in enumerate(rows))
    peers, n_tok = out_ref.shape[0], out_ref.shape[1] - 8
    stats = jnp.concatenate(_thirds(top) + _thirds(total) + _thirds(hit) + [jnp.zeros((7, tokens), F32)], axis=0)
    stats = pltpu.roll(stats, lax.rem(z + peers - 1, peers) * n_tok, 1)
    pairs = [jnp.concatenate([stats[2 * k : 2 * k + 1], stats[2 * k + 1 : 2 * k + 2]], axis=1) for k in range(8)]
    stats = jnp.concatenate(pairs, axis=0)
    stats = jnp.concatenate([stats, jnp.zeros((8, 2 * feats - 2 * tokens), F32)], axis=1).astype(BF16)
    for p in range(peers):
        out_ref[lax.rem(z + p + peers - 1, peers), :n_tok] = both[p * n_tok : (p + 1) * n_tok]
        out_ref[p, n_tok:] = stats


def _finish_kernel(pos_ref, got, grad_ref, stat_ref, turned):
    peers, span, _ = got.shape
    n_tok, feats = grad_ref.shape
    tokens = stat_ref.shape[1]
    wide = [got[r, n_tok:, : 2 * tokens].astype(F32) for r in range(peers)]
    ends = [[w[k // 2 : k // 2 + 1, k % 2 * tokens : (k % 2 + 1) * tokens] for k in range(9)] for w in wide]
    tops = [e[0] + e[1] + e[2] for e in ends]
    top = functools.reduce(jnp.maximum, tops)
    scales = [jnp.exp(t - top) for t in tops]
    total = sum((e[3] + e[4] + e[5]) * f for e, f in zip(ends, scales))
    hit = sum(e[6] + e[7] + e[8] for e in ends)
    stat_ref[...] = jnp.concatenate([top, total, hit, jnp.zeros((5, tokens), F32)], axis=0)
    inv = 1.0 / total
    rows = [f * inv for f in scales] + [jnp.exp(hit - top) * inv - 1.0, jnp.zeros((128 - peers - 1, tokens), F32)]
    turned[...] = jnp.concatenate(rows, axis=0).T
    own = turned[pl.ds(pl.multiple_of(pos_ref[0] * n_tok, n_tok), n_tok)]
    grad, targets = 0.0, 0.0
    for r in range(peers):
        block = got[r, :n_tok].astype(F32)
        grad += block[:, :feats] * own[:, r : r + 1]
        targets += block[:, feats:]
    grad_ref[...] = (grad + targets * own[:, peers : peers + 1]).astype(BF16)


def _grad_table_kernel(pos_ref, tok_ref, tgt_own, tgt_oth, stat_own, stat_oth, *refs):
    own_a, own_b, oth_a, oth_b, h_own_a, h_own_b, h_oth_a, h_oth_b, e_ref, out_ref, loss_ref, dl, hot = refs

    @pl.when(pl.program_id(0) == 0)
    def _():
        rows, tokens = own_a.shape[0], tgt_own.shape[1]
        at = lax.broadcasted_iota(jnp.int32, hot.shape, 0) + pos_ref[1]
        hot[...] = jnp.where(at == tok_ref[...], 1.0, 0.0).astype(BF16)
        turn = lax.rem(9 - pos_ref[0], 8) * (tokens // 8)
        losses = []
        for k, (tgt, stat, a, b) in enumerate(((tgt_own, stat_own, own_a, own_b), (tgt_oth, stat_oth, oth_a, oth_b))):
            losses.append(jnp.sum(stat[0:1] + jnp.log(stat[1:2]) - stat[2:3], keepdims=True))
            turned = pltpu.roll(stat[...], turn, 1)
            hit = jnp.where(at[:, :tokens] == tgt[...], 1.0, 0.0)
            logit = jnp.concatenate([a[...], b[...]], axis=1)
            dl[k] = (jnp.exp(logit - turned[0:1]) * (1.0 / turned[1:2]) - hit).astype(BF16)
        loss_ref[...] = losses[0] + losses[1]

    acc = jnp.dot(hot[...], e_ref[...], preferred_element_type=F32)
    acc += jnp.dot(dl[0], jnp.concatenate([h_own_a[...], h_own_b[...]], axis=0), preferred_element_type=F32)
    acc += jnp.dot(dl[1], jnp.concatenate([h_oth_a[...], h_oth_b[...]], axis=0), preferred_element_type=F32)
    out_ref[...] = acc.astype(BF16)


def per_device(hidden, table, embed_grad, token_ids, target_ids):
    rows, width = table.shape
    n_tok = hidden.shape[0]
    nz, nxy = lax.axis_size("z"), lax.axis_size(XY)
    feats = width // nxy
    tokens = n_tok * nz
    xi, yi, zi, ci = (lax.axis_index(a) for a in ALL)
    chip = (xi * 4 + yi) * nz + zi
    swap = [(0, 1), (1, 0)]
    up = [(i, (i + 1) % nz) for i in range(nz)]
    down = [(i, (i - 1) % nz) for i in range(nz)]
    smem = pl.BlockSpec(memory_space=pltpu.SMEM)
    vmem = pl.BlockSpec(memory_space=pltpu.VMEM)
    hbm = pl.BlockSpec(memory_space=pl.ANY)

    def far_off(x):
        return pltpu.with_memory_space_constraint(x, pltpu.HBM)

    def pos_of(first):
        return jnp.stack([zi, (2 * chip + ci) * rows, (2 * chip + 1 - ci) * rows, first]).astype(jnp.int32)

    pos = pos_of(0)
    table_oth = lax.ppermute(table, "c", swap)
    ids = jnp.concatenate([target_ids, token_ids])
    ids = lax.all_to_all(jnp.broadcast_to(ids[None], (2 * nz, 2 * n_tok)), ("z", "c"), 0, 0, tiled=True)

    u, d = lax.optimization_barrier((lax.ppermute(hidden, "z", up), lax.ppermute(hidden, "z", down)))
    ups, downs = [u], [d]
    u, d, ids = lax.optimization_barrier((lax.ppermute(u, "z", up), lax.ppermute(d, "z", down), ids))
    ups.append(u)
    downs.append(d)

    both = ids[:, :n_tok].reshape(nz, 2, n_tok).transpose(1, 0, 2)
    both = jnp.roll(both, 1 - zi, axis=1).reshape(2, tokens)
    part_of = jnp.arange(tokens) // (tokens // 2)
    alike = part_of[:, None] == part_of[None, :]
    before = jnp.arange(tokens)[:, None] < jnp.arange(tokens)[None, :]
    same = both[:, :, None] == both[:, None, :]
    fresh = ~jnp.any(same & (alike & before)[None], axis=1)
    owner = both // (2 * rows)
    below = (owner[:, :, None] == owner[:, None, :]) & (both[:, :, None] < both[:, None, :]) & alike[None] & fresh[:, :, None]
    ranks = jnp.sum(below, axis=1).astype(jnp.int32)
    overflow = jnp.max(ranks) >= SLOTS
    targets = lax.dynamic_index_in_dim(both, ci, 0)
    targets_oth = lax.dynamic_index_in_dim(both, 1 - ci, 0)
    rank = lax.dynamic_index_in_dim(ranks, ci, 0)
    owner = targets // (2 * rows)
    here = owner % nz == zi
    place = jnp.where(here & (rank < SLOTS), owner // nz * SLOTS + rank, -1)
    toks = ids[:, n_tok:].reshape(1, 2 * tokens)

    def round_of(first, part):
        rank_in = jnp.where(part_of[None] == part, rank, -1)
        width_q = 2 * feats
        row = pl.BlockSpec((1, tokens), lambda i: (0, 0))
        sent = pl.pallas_call(
            functools.partial(_target_rows_kernel, rows),
            grid=(width // width_q,),
            in_specs=[smem, row, row, *[pl.BlockSpec((rows, width_q), lambda i: (0, i))] * 2],
            out_specs=pl.BlockSpec((2, MORE_SLOTS, feats), lambda i: (i, 0, 0)),
            out_shape=jax.ShapeDtypeStruct((nxy, MORE_SLOTS, feats), BF16),
            scratch_shapes=[pltpu.VMEM((MORE_SLOTS, 2 * rows), BF16)],
            compiler_params=_params(),
            cost_estimate=_cost(4 * rows * MORE_SLOTS * width, 4 * rows * width),
            name="target_rows",
        )(pos_of(first), targets, rank_in, table, table_oth)
        got = lax.all_to_all(sent, XY, 0, 0, tiled=True).reshape(nxy * MORE_SLOTS, feats)
        inside = here & (rank_in >= first) & (rank_in < first + MORE_SLOTS)
        slot = jnp.where(inside, owner // nz * MORE_SLOTS + rank_in - first, -1)
        hot = (jnp.arange(nxy * MORE_SLOTS, dtype=jnp.int32)[:, None] == slot).astype(BF16)
        return lax.dot_general(got, hot, TN, preferred_element_type=F32)

    def more():
        return sum(round_of(first, part) for part in range(2) for first in range(SLOTS, tokens // 2, MORE_SLOTS))

    span = feats + 3 * SLOTS + 8
    wide = tokens // 2

    def forward(name, part, share, *pieces):
        cut = slice(part * wide, (part + 1) * wide)
        return pl.pallas_call(
            functools.partial(_forward_kernel, rows),
            in_specs=[smem, vmem, vmem] + [hbm] * (2 + len(pieces)),
            out_specs=[hbm] * 3,
            out_shape=[
                pltpu.HBM((2 * rows, wide), F32),
                pltpu.HBM((wide, width), BF16),
                pltpu.HBM((nxy, span, wide), BF16),
            ],
            scratch_shapes=[
                pltpu.VMEM((2 * rows, wide), F32),
                pltpu.VMEM((2, rows, width), BF16),
                pltpu.VMEM((wide, width), BF16),
                pltpu.VMEM((nxy, span, wide), BF16),
                pltpu.SemaphoreType.DMA((len(pieces) + 2 * (width // WIDE) + 2 + nxy // 2,)),
            ],
            compiler_params=_params(),
            cost_estimate=_cost(8 * rows * wide * width // share, (4 * rows * width + 6 * wide * width) // share),
            name=name,
        )(pos, targets[:, cut], rank[:, cut], table, table_oth, *pieces)

    half = n_tok // 2
    far = (
        lax.ppermute(u[:half], "z", [(i, (i + 2) % nz) for i in range(nz)]),
        lax.ppermute(d[half:], "z", [(i, (i - 2) % nz) for i in range(nz)]),
    )
    u, d = lax.ppermute(u, "z", up), lax.ppermute(d, "z", down)
    logit_a, h_own_a, part_a = forward("forward_a", 0, 1, ups[0], far_off(hidden), downs[0], downs[1])
    u, d, *far, part_a = lax.optimization_barrier((u, d, *far, part_a))
    got_a = lax.all_to_all(part_a, XY, 0, 0, tiled=True)
    logit_b, h_own_b, part_b = forward("forward_b", 1, 1, d, *far, u, ups[1])
    got_b = lax.all_to_all(part_b, XY, 0, 0, tiled=True)

    e_src, _ = lax.optimization_barrier((embed_grad, u))
    e_all = lax.all_gather(e_src, ("z", "c"), axis=0, tiled=True)

    h_oth_a, h_oth_b, oth_a, oth_b = (
        lax.ppermute(v, "c", swap) for v in (h_own_a, h_own_b, logit_a[rows:], logit_b[rows:])
    )
    sums_a, stat_a = pl.pallas_call(
        _half_kernel,
        in_specs=[vmem] * 2,
        out_specs=[vmem] * 2,
        out_shape=[jax.ShapeDtypeStruct((wide, 2 * feats), BF16), jax.ShapeDtypeStruct((8, wide), F32)],
        compiler_params=_params(),
        cost_estimate=_cost(10**6, 10**5),
        name="half",
    )(place[:, :wide], got_a)
    overflow, sums_a, got_b = lax.optimization_barrier((overflow, sums_a, got_b))
    q_more = lax.cond(overflow, more, lambda: jnp.zeros((feats, tokens), F32))
    by_z = pl.pallas_call(
        _combine_kernel,
        in_specs=[smem] + [vmem] * 5,
        out_specs=vmem,
        out_shape=jax.ShapeDtypeStruct((nz, n_tok + 8, 2 * feats), BF16),
        compiler_params=_params(),
        cost_estimate=_cost(10**6, 10**5),
        name="combine",
    )(pos, place[:, wide:], q_more, got_b, sums_a, stat_a)
    by_z = lax.all_to_all(by_z, "z", 0, 0, tiled=True)

    grad_hidden, stat = pl.pallas_call(
        _finish_kernel,
        in_specs=[smem, vmem],
        out_specs=[vmem, vmem],
        out_shape=[jax.ShapeDtypeStruct((n_tok, feats), BF16), jax.ShapeDtypeStruct((8, tokens), F32)],
        scratch_shapes=[pltpu.VMEM((tokens, 128), F32)],
        compiler_params=_params(),
        cost_estimate=_cost(10**6, 10**5),
        name="finish",
    )(pos, by_z)
    stat_oth = lax.ppermute(stat, "c", swap)

    whole = lambda *shape: pl.BlockSpec(shape, lambda i: (0,) * len(shape))
    col = lambda n: pl.BlockSpec((n, TABLE_WIDE), lambda i: (0, i))
    grad_table, loss = pl.pallas_call(
        _grad_table_kernel,
        grid=(width // TABLE_WIDE,),
        in_specs=[smem, whole(1, 2 * tokens), *[whole(1, tokens)] * 2, *[whole(8, tokens)] * 2, *[whole(rows, wide)] * 4]
        + [col(wide)] * 4
        + [col(2 * tokens)],
        out_specs=[col(rows), whole(1, 1)],
        out_shape=[jax.ShapeDtypeStruct((rows, width), BF16), jax.ShapeDtypeStruct((1, 1), F32)],
        scratch_shapes=[pltpu.VMEM((2, rows, tokens), BF16), pltpu.VMEM((rows, 2 * tokens), BF16)],
        compiler_params=_params(),
        cost_estimate=_cost(8 * rows * tokens * width, 8 * tokens * width + 2 * rows * width),
        name="grad_table",
    )(pos, toks, targets, targets_oth, stat, stat_oth, logit_a, logit_b, oth_a, oth_b, *map(far_off, (h_own_a, h_own_b, h_oth_a, h_oth_b, e_all)))
    return grad_hidden, grad_table, loss[0, 0]


def solution(mesh):
    fine = Mesh(mesh.devices.reshape(4, 4, 8, 2), ALL)
    in_specs = (P(("z", "c"), None), P(ALL, None), P(("z", "c"), None), P(("z", "c")), P(("z", "c")))
    out_specs = (P(("z", "c"), XY), P(ALL, None), P())
    return jax.shard_map(per_device, mesh=fine, in_specs=in_specs, out_specs=out_specs, check_vma=False)
```
